32 devices in a mesh: src: 8 (over z, y), tgt: 4 (over x, core).
Axes of the slice: x: 2, y: 2, z: 4, core: 2. Of those that a mesh axis runs over, the one named last changes fastest.
Arguments:
- text_emb: bfloat16 [16384, 512], P('src'), may hold values from -32 to 32
- image_emb: bfloat16 [8192, 512], P('tgt'), may hold values from -12 to 12
- log_mass_src: float32 [16384], P('src'), may hold values from -1 to 1
- log_mass_tgt: float32 [8192], P('tgt'), may hold values from -1 to 1
- pair_blocks: int32 [512, 2], P(('src', 'tgt')), may hold values from 0 to 7, as said below
- pair_counts: int32 [32], P(('src', 'tgt')), may hold values from 2 to 16, as said below
Outputs:
- src_map: float32 [16384, 512], P(('src', 'tgt'))
- tgt_map: float32 [8192, 512], P(('tgt', 'src'))
The draws below stay inside these ranges and needn't reach their ends.
Inputs may be any that keep to these rules, and one draw needn't show every extreme that they name: `pair_blocks`: column 0 is a local text cluster below 8, column 1 a local image cluster below 8. The first pair_counts slots of a device hold distinct pairs; every text cluster and every image cluster lies in some used slot. Unused slots hold valid indices that are ignored. `pair_counts`: at least 8 // 4 used slots on every device; some device uses all 16 in every draw.
All inputs are finite; a program needn't handle non-finite values.
Results may differ from the reference program's by a relative error of at most 0.0028.
Values sent between devices are 32-bit elements; how exact they have to be, the bound alone decides.
A program may use at most 64 MiB of HBM per device.

```python
import jax
import jax.numpy as jnp
from jax import lax

D = 512
BLK = 256
SB_DEV = 8
TB_GRP = 8
ITERS = 3
PAIR_CAP = 16
NS = 16384
NT = 8192
N_SRC = 8
N_TGT = 4


def pair_layout(key):
    base = jax.random.fold_in(key, 7)
    ndevices = N_SRC * N_TGT
    each = SB_DEV // N_TGT
    combos = SB_DEV * TB_GRP
    device_ids = jnp.arange(ndevices, dtype=jnp.int32)
    src_index = device_ids // N_TGT
    tgt_index = device_ids % N_TGT
    rank = jnp.arange(each, dtype=jnp.int32)
    sure_src = tgt_index[:, None] + N_TGT * rank[None, :]
    sure_tgt = (src_index[:, None] * each + rank[None, :]) % TB_GRP
    sure_combo = sure_src * TB_GRP + sure_tgt
    noise = jax.random.randint(jax.random.fold_in(base, 1), (ndevices, combos), 0, 1 << 20)
    combo_ids = jnp.arange(combos, dtype=jnp.int32)
    score = noise * combos + combo_ids[None, :]
    hit = (combo_ids[None, None, :] == sure_combo[:, :, None]).any(axis=1)
    score = score + jnp.where(hit, 1 << 30, 0)
    _, chosen = lax.top_k(score, PAIR_CAP)
    draws = jax.random.randint(jax.random.fold_in(base, 2), (ndevices,), 0, PAIR_CAP)
    extra = jnp.minimum(draws * draws // (PAIR_CAP - 2), PAIR_CAP - each)
    counts = each + extra
    busiest = jax.random.randint(jax.random.fold_in(base, 3), (), 0, ndevices)
    counts = jnp.where(device_ids == busiest, PAIR_CAP, counts)
    blocks = jnp.stack([chosen // TB_GRP, chosen % TB_GRP], axis=-1).reshape(ndevices * PAIR_CAP, 2)
    return (blocks.astype(jnp.int32), counts.astype(jnp.int32))


def draw_pair_blocks(key, part):
    return pair_layout(key)[0]


def draw_pair_counts(key, part):
    return pair_layout(key)[1]


def draw_text_emb(key, part):
    rows = SB_DEV * BLK * N_SRC
    values = jax.random.truncated_normal(jax.random.fold_in(key, 5), -4.0, 4.0, (rows, D), jnp.float32)
    return values.astype(jnp.bfloat16)


def draw_image_emb(key, part):
    rows = TB_GRP * BLK * N_TGT
    values = jax.random.truncated_normal(jax.random.fold_in(key, 9), -4.0, 4.0, (rows, D), jnp.float32)
    return values.astype(jnp.bfloat16)


def shard_levels(key, extent, shards, least, top_value):
    level, own = 1.0, jax.random.fold_in(key, 6)
    for position, blocks in shards:
        steps = jnp.exp(jax.random.uniform(jax.random.fold_in(own, position), (blocks,), jnp.float32, least / len(shards), top_value / len(shards)))
        level = level * jnp.repeat(steps, extent[position] // blocks).reshape([-1 if axis == position else 1 for axis in range(len(extent))])
    return level


def setup_inputs(seed: int = 0) -> dict:
    streams_of = jax.random.split(jax.random.key(seed), 7)
    text_emb = draw_text_emb(jax.random.fold_in(streams_of[6], 71), 0)
    image_emb = draw_image_emb(jax.random.fold_in(streams_of[6], 71), 0)
    log_mass_src = jnp.clip(jax.random.uniform(streams_of[2], (NS,), jnp.float32, -1.0, 1.0) * shard_levels(streams_of[2], (NS,), ((0, 8),), -0.4, 0.0), -1.0, 1.0)
    log_mass_tgt = jnp.clip(jax.random.uniform(streams_of[3], (NT,), jnp.float32, -1.0, 1.0) * shard_levels(streams_of[3], (NT,), ((0, 4),), -0.4, 0.0), -1.0, 1.0)
    pair_blocks = draw_pair_blocks(jax.random.fold_in(streams_of[6], 71), 0)
    pair_counts = draw_pair_counts(jax.random.fold_in(streams_of[6], 71), 0)
    return dict(text_emb=text_emb, image_emb=image_emb, log_mass_src=log_mass_src, log_mass_tgt=log_mass_tgt, pair_blocks=pair_blocks, pair_counts=pair_counts)


inv_temp = 0.15
floor_value = -1e30


def reference(text_emb, image_emb, log_mass_src, log_mass_tgt, pair_blocks, pair_counts):
    total = N_SRC * N_TGT * PAIR_CAP
    slot_ids = jnp.arange(total, dtype=jnp.int32)
    device_ids = slot_ids // PAIR_CAP
    valid = (slot_ids % PAIR_CAP) < pair_counts[device_ids]
    src_blk = ((device_ids // N_TGT) * SB_DEV + pair_blocks[:, 0]).astype(jnp.int32)
    tgt_blk = ((device_ids % N_TGT) * TB_GRP + pair_blocks[:, 1]).astype(jnp.int32)
    src_count = SB_DEV * N_SRC
    tgt_count = TB_GRP * N_TGT
    text_blocks = text_emb.reshape(src_count, BLK, D)
    image_blocks = image_emb.reshape(tgt_count, BLK, D)

    def score_tile(index):
        return jnp.dot(text_blocks[index[0]], image_blocks[index[1]].T, preferred_element_type=jnp.float32) * inv_temp

    tiles = lax.map(score_tile, (src_blk, tgt_blk))
    mask = valid[:, None, None]
    mass_src = log_mass_src.reshape(src_count, BLK)
    mass_tgt = log_mass_tgt.reshape(tgt_count, BLK)
    tgt_pot = jnp.zeros((tgt_count, BLK), jnp.float32)
    src_pot = jnp.zeros((src_count, BLK), jnp.float32)
    for step in range(ITERS):
        shifted = jnp.where(mask, tiles + tgt_pot[tgt_blk][:, None, :], floor_value)
        peak = jnp.full((src_count, BLK), floor_value, jnp.float32).at[src_blk].max(shifted.max(axis=2))
        sums = jnp.zeros((src_count, BLK), jnp.float32).at[src_blk].add(
            jnp.exp(shifted - peak[src_blk][:, :, None]).sum(axis=2))
        src_pot = mass_src - peak - jnp.log(sums)
        shifted = jnp.where(mask, tiles + src_pot[src_blk][:, :, None], floor_value)
        peak = jnp.full((tgt_count, BLK), floor_value, jnp.float32).at[tgt_blk].max(shifted.max(axis=1))
        sums = jnp.zeros((tgt_count, BLK), jnp.float32).at[tgt_blk].add(
            jnp.exp(shifted - peak[tgt_blk][:, None, :]).sum(axis=1))
        tgt_pot = mass_tgt - peak - jnp.log(sums)
    plan = jnp.where(mask, jnp.exp(tiles + src_pot[src_blk][:, :, None] + tgt_pot[tgt_blk][:, None, :]), 0.0)
    row_mass = jnp.zeros((src_count, BLK), jnp.float32).at[src_blk].add(plan.sum(axis=2))
    col_mass = jnp.zeros((tgt_count, BLK), jnp.float32).at[tgt_blk].add(plan.sum(axis=1))
    weights = plan.astype(jnp.bfloat16)

    def accumulate(carry, item):
        src_numer, tgt_numer = carry
        weight, src_index, tgt_index = item
        src_numer = src_numer.at[src_index].add(
            jnp.dot(weight, image_blocks[tgt_index], preferred_element_type=jnp.float32))
        tgt_numer = tgt_numer.at[tgt_index].add(
            jnp.dot(weight.T, text_blocks[src_index], preferred_element_type=jnp.float32))
        return (src_numer, tgt_numer), None

    start = (jnp.zeros((src_count, BLK, D), jnp.float32), jnp.zeros((tgt_count, BLK, D), jnp.float32))
    (src_numer, tgt_numer), _ = lax.scan(accumulate, start, (weights, src_blk, tgt_blk))
    src_map = (src_numer / row_mass[:, :, None]).reshape(NS, D)
    tgt_map = (tgt_numer / col_mass[:, :, None]).reshape(NT, D)
    return (src_map, tgt_map)
```

```python
import functools

import jax
import jax.numpy as jnp
from jax import lax
from jax.experimental import pallas as pl
from jax.experimental.pallas import tpu as pltpu
from jax.sharding import PartitionSpec as P

BLK = 256
ITERS = 3
LANES = 128

inv_temp = 0.15
floor_value = -1e30
MESH = pl.DeviceIdType.MESH


def each(low, high, body):
    if high - low <= 8:
        for i in range(low, high):
            body(i)
    else:

        def step(i, carry):
            body(i)
            return carry

        lax.fori_loop(low, high, step, 0)


def looped(low, high, body, unroll=1):

    def step(i, carry):
        body(i)
        return carry

    lax.fori_loop(low, high, step, 0, unroll=unroll)


def partner(me, n, step):
    if n & (n - 1):
        return lax.rem(me + 1 + step, n)
    mask = n - 1 - step
    out = me * 0
    bit = 1
    while bit < n:
        out = out + ((me // bit + mask // bit) % 2) * bit
        bit *= 2
    return out


def kernel(
    n_src, n_tgt, inner,
    pairs, count, slots, text, image, mass_src, mass_tgt,
    src_out, tgt_out,
    score, score_t, weight, weight_t, bias_src, bias_tgt,
    src_wide, tgt_wide, src_row, tgt_row, top, tot,
    src_parts, tgt_parts,
    pair_send, pair_got, outer_sum, outer_got, part_send, part_got,
    src_ss, src_rs, tgt_ss, tgt_rs,
    pair_ss, pair_rs, outer_ss, outer_rs, part_ss, part_rs,
):
    cap = score.shape[0]
    sb, block, width = text.shape
    tb = image.shape[0]
    s = lax.axis_index("src")
    t = lax.axis_index("tgt")
    n_outer = n_src // inner
    outer, side = s // inner, s % inner
    mate = outer * inner + (inner - 1 - side)

    def greet(device):
        pl.semaphore_signal(barrier, inc=1, device_id=device, device_id_type=MESH)

    barrier = pltpu.get_barrier_semaphore()
    each(1, n_tgt, lambda d: greet((s, (t + d) % n_tgt)))
    each(1, n_src, lambda d: greet(((s + d) % n_src, t)))

    def make_bias(k):
        used = k < count[0]
        rows = lax.broadcasted_iota(jnp.int32, (sb, block), 0)
        a = jnp.where(used, pairs[k, 0], -1)
        bias_src[k] = jnp.where(rows == a, 0.0, floor_value)
        cols = lax.broadcasted_iota(jnp.int32, (tb, block), 0)
        b = jnp.where(used, pairs[k, 1], -1)
        bias_tgt[k] = jnp.where(cols == b, 0.0, floor_value)

    def make_scores(k):
        make_bias(k)
        rows, cols = text[pairs[k, 0]], image[pairs[k, 1]]
        nt = (((1,), (1,)), ((), ()))
        score[k] = lax.dot_general(rows, cols, nt, preferred_element_type=jnp.float32) * inv_temp
        score_t[k] = lax.dot_general(cols, rows, nt, preferred_element_type=jnp.float32) * inv_temp

    looped(0, cap, make_scores)
    tgt_wide[...] = jnp.zeros_like(tgt_wide)
    pl.semaphore_wait(barrier, n_tgt - 1 + n_src - 1)

    def push(parts, step, me, n, device, ss, rs, d):
        return pltpu.make_async_remote_copy(
            src_ref=parts.at[step, me],
            dst_ref=parts.at[step, me],
            send_sem=ss.at[step, d],
            recv_sem=rs.at[step, me],
            device_id=device,
            device_id_type=MESH,
        )

    def arrival(parts, step, d, me, n, device, ss, rs):
        other = (me + d) % n
        return pltpu.make_async_remote_copy(
            src_ref=parts.at[step, other],
            dst_ref=parts.at[step, other],
            send_sem=ss.at[step, d],
            recv_sem=rs.at[step, other],
            device_id=device,
            device_id_type=MESH,
        )

    def src_group(d):
        return (s, (t + d) % n_tgt)

    def tgt_group(d):
        return ((s + d) % n_src, t)

    sides = {
        "src": (src_parts, t, n_tgt, src_group, src_ss, src_rs),
        "tgt": (tgt_parts, s, n_src, tgt_group, tgt_ss, tgt_rs),
    }

    def send_parts(which, step):
        parts, me, n, group, ss, rs = sides[which]
        each(1, n, lambda d: push(parts, step, me, n, group(d), ss, rs, d).start())

    def wait_parts(which, step):
        parts, me, n, group, ss, rs = sides[which]
        each(1, n, lambda d: arrival(parts, step, d, me, n, group(d), ss, rs).wait_recv())
        each(1, n, lambda d: push(parts, step, me, n, group(d), ss, rs, d).wait_send())

    def lse_pass(tiles, wide, column):

        def one(k):
            shift = wide[pairs[k, column]]
            for h in range(block // LANES):
                lanes = pl.ds(h * LANES, LANES)
                shifted = (tiles[k, :, lanes] + shift).reshape(block // 8, 8, LANES)
                peak = jnp.max(shifted, axis=0)
                top[k, :, lanes] = peak
                tot[k, :, lanes] = jnp.sum(jnp.exp(shifted - peak[None]), axis=0)

        looped(0, cap, one, unroll=2)

    def local_part(bias):
        peaks = top[...]
        peak = jnp.max(peaks, axis=1, keepdims=True)
        total = jnp.sum(tot[...] * jnp.exp(peaks - peak), axis=1, keepdims=True)
        masked = (peak + jnp.log(total)) + bias[...]
        highest = jnp.max(masked, axis=0)
        return highest + jnp.log(jnp.sum(jnp.exp(masked - highest[None]), axis=0))

    def merged(parts, step):
        every = parts[step]
        highest = jnp.max(every, axis=0)
        return highest + jnp.log(jnp.sum(jnp.exp(every - highest[None]), axis=0))

    def widen(value, wide):
        columns = value.T
        for c in range(value.shape[0]):
            wide[c] = jnp.broadcast_to(columns[:, c : c + 1], (block, LANES))

    def spread(value, row):
        for c in range(value.shape[0]):
            row[c] = value[c : c + 1, :]

    def iterate(step):
        lse_pass(score_t, tgt_wide, 1)
        src_parts[step, t] = local_part(bias_src)
        send_parts("src", step)
        wait_parts("src", step)
        pot = mass_src[...] - merged(src_parts, step)
        widen(pot, src_wide)
        spread(pot, src_row)
        lse_pass(score, src_wide, 0)
        tgt_parts[step, s] = local_part(bias_tgt)
        send_parts("tgt", step)
        wait_parts("tgt", step)
        pot = mass_tgt[...] - merged(tgt_parts, step)
        widen(pot, tgt_wide)
        spread(pot, tgt_row)

    looped(0, ITERS, iterate)

    def plan(k):
        a, b = pairs[k, 0], pairs[k, 1]
        for h in range(block // LANES):
            lanes = pl.ds(h * LANES, LANES)
            tile = score[k, :, lanes] + src_wide[a] + tgt_row[b, :, lanes]
            tile = jnp.exp(tile)
            weight[k, :, lanes] = tile.astype(jnp.bfloat16)
            top[k, :, lanes] = jnp.sum(tile.reshape(block // 8, 8, LANES), axis=0)
            tile = score_t[k, :, lanes] + src_row[a, :, lanes] + tgt_wide[b]
            tile = jnp.exp(tile)
            weight_t[k, :, lanes] = tile.astype(jnp.bfloat16)
            tot[k, :, lanes] = jnp.sum(tile.reshape(block // 8, 8, LANES), axis=0)

    looped(0, cap, plan)
    weight[cap] = jnp.zeros(weight.shape[1:], weight.dtype)
    weight_t[cap] = jnp.zeros(weight_t.shape[1:], weight_t.dtype)

    def mass_part(sums, bias):
        rows = jnp.sum(sums[...], axis=1, keepdims=True)
        return jnp.sum(jnp.where(bias[...] == 0.0, rows, 0.0), axis=0)

    src_parts[ITERS, t] = mass_part(tot, bias_src)
    tgt_parts[ITERS, s] = mass_part(top, bias_tgt)
    send_parts("tgt", ITERS)
    send_parts("src", ITERS)

    def unit_rows(n, clusters):
        own = clusters * block // n
        return own, min(own, block)

    tgt_own, tgt_unit = unit_rows(n_src, tb)
    src_own, src_unit = unit_rows(n_tgt, sb)

    def numer(start, unit, tiles, index, count_other, table):
        cluster, off = start // block, start % block
        picks = []
        for c in range(count_other):
            slot = slots[index(cluster, c)]
            if unit == block:
                picks.append(tiles[slot])
            else:
                picks.append(tiles[slot, pl.ds(pl.multiple_of(off, unit), unit), :])
        left = jnp.concatenate(picks, axis=1)
        right = table[...].reshape(count_other * block, width)
        return jnp.dot(left, right, preferred_element_type=jnp.float32)

    def tgt_numer(owner, out, where):
        for u in range(tgt_own // tgt_unit):
            start = owner * tgt_own + u * tgt_unit
            out[where, pl.ds(u * tgt_unit, tgt_unit), :] = numer(
                start, tgt_unit, weight_t, lambda j, a: a * tb + j, sb, text
            )

    def src_numer(owner, out, where):

        def unit(u):
            start = owner * src_own + u * src_unit
            rows = pl.ds(pl.multiple_of(u * src_unit, src_unit), src_unit)
            out[where, rows, :] = numer(start, src_unit, weight, lambda i, b: i * tb + b, tb, image)

        looped(0, src_own // src_unit, unit)

    def pair_copy(z):
        return pltpu.make_async_remote_copy(
            src_ref=pair_send.at[z],
            dst_ref=pair_got.at[z],
            send_sem=pair_ss.at[z],
            recv_sem=pair_rs.at[z],
            device_id=(mate, t),
            device_id_type=MESH,
        )

    def outer_copy(z, slot):
        return pltpu.make_async_remote_copy(
            src_ref=outer_sum.at[z],
            dst_ref=outer_got.at[slot],
            send_sem=outer_ss.at[z],
            recv_sem=outer_rs.at[slot],
            device_id=(z * inner + side, t),
            device_id_type=MESH,
        )

    def part_copy(other, slot):
        return pltpu.make_async_remote_copy(
            src_ref=part_send.at[other],
            dst_ref=part_got.at[slot],
            send_sem=part_ss.at[other],
            recv_sem=part_rs.at[slot],
            device_id=(s, other),
            device_id_type=MESH,
        )

    def to_mate(step):
        z = partner(outer, n_outer, step)
        tgt_numer(z * inner + (inner - 1 - side), pair_send, z)
        pair_copy(z).start()

    def to_part(step):
        other = partner(t, n_tgt, step)
        src_numer(other, part_send, other)
        part_copy(other, t).start()

    def own_outer(step):
        z = partner(outer, n_outer, step)
        tgt_numer(z * inner + side, outer_sum, z)

    if inner == 2:
        looped(0, n_outer, to_mate)
    looped(0, n_tgt - 1, to_part)
    looped(0, n_outer, own_outer)

    def forward(step):
        z = partner(outer, n_outer, step)
        if inner == 2:
            pair_copy(z).wait_recv()
            outer_sum[z] = outer_sum[z] + pair_got[z]
        outer_copy(z, outer).start()

    looped(0, n_outer - 1, forward)
    src_numer(t, part_send, t)

    wait_parts("src", ITERS)
    wait_parts("tgt", ITERS)
    widen(jnp.sum(src_parts[ITERS], axis=0), src_wide)
    widen(jnp.sum(tgt_parts[ITERS], axis=0), tgt_wide)

    def take_part(step):
        other = partner(t, n_tgt, step)
        part_copy(other, other).wait_recv()
        part_send[t] = part_send[t] + part_got[other]

    looped(0, n_tgt - 1, take_part)
    for u in range(src_own // src_unit):
        start = t * src_own + u * src_unit
        rows = pl.ds(u * src_unit, src_unit)
        off = pl.multiple_of(start % block, src_unit)
        mass = src_wide[start // block, pl.ds(off, src_unit), :]
        for c in range(width // LANES):
            lanes = pl.ds(c * LANES, LANES)
            src_out[rows, lanes] = part_send[t, rows, lanes] / mass

    if inner == 2:
        pair_copy(outer).wait_recv()
        outer_sum[outer] = outer_sum[outer] + pair_got[outer]

    def take_outer(step):
        z = partner(outer, n_outer, step)
        outer_copy(z, z).wait_recv()
        outer_sum[outer] = outer_sum[outer] + outer_got[z]

    looped(0, n_outer - 1, take_outer)
    for u in range(tgt_own // tgt_unit):
        start = s * tgt_own + u * tgt_unit
        rows = pl.ds(u * tgt_unit, tgt_unit)
        off = pl.multiple_of(start % block, tgt_unit)
        mass = tgt_wide[start // block, pl.ds(off, tgt_unit), :]
        for c in range(width // LANES):
            lanes = pl.ds(c * LANES, LANES)
            tgt_out[rows, lanes] = outer_sum[outer, rows, lanes] / mass

    def sent_pair(step):
        pair_copy(partner(outer, n_outer, step)).wait_send()

    def sent_outer(step):
        outer_copy(partner(outer, n_outer, step), outer).wait_send()

    def sent_part(step):
        part_copy(partner(t, n_tgt, step), t).wait_send()

    if inner == 2:
        looped(0, n_outer, sent_pair)
    looped(0, n_outer - 1, sent_outer)
    looped(0, n_tgt - 1, sent_part)


def local(n_src, n_tgt, text_emb, image_emb, log_mass_src, log_mass_tgt, pair_blocks, pair_counts):
    sb = text_emb.shape[0] // BLK
    tb = image_emb.shape[0] // BLK
    width = text_emb.shape[1]
    cap = pair_blocks.shape[0]
    inner = 2 if n_src % 2 == 0 else 1
    n_outer = n_src // inner
    tgt_own = tb * BLK // n_src
    src_own = sb * BLK // n_tgt

    slot_ids = jnp.arange(cap, dtype=jnp.int32)
    combo = jnp.where(slot_ids < pair_counts[0], pair_blocks[:, 0] * tb + pair_blocks[:, 1], -1)
    combos = jnp.arange(sb * tb, dtype=jnp.int32)
    slots = jnp.min(jnp.where(combo[None, :] == combos[:, None], slot_ids[None, :], cap), axis=1)

    f32, bf16 = jnp.float32, jnp.bfloat16
    dma = pltpu.SemaphoreType.DMA
    smem = pl.BlockSpec(memory_space=pltpu.SMEM)
    vmem = pl.BlockSpec(memory_space=pltpu.VMEM)
    return pl.pallas_call(
        functools.partial(kernel, n_src, n_tgt, inner),
        out_shape=(
            jax.ShapeDtypeStruct((src_own, width), f32),
            jax.ShapeDtypeStruct((tgt_own, width), f32),
        ),
        in_specs=[smem] * 3 + [vmem] * 4,
        out_specs=(vmem, vmem),
        scratch_shapes=[
            pltpu.VMEM((cap, BLK, BLK), f32),
            pltpu.VMEM((cap, BLK, BLK), f32),
            pltpu.VMEM((cap + 1, BLK, BLK), bf16),
            pltpu.VMEM((cap + 1, BLK, BLK), bf16),
            pltpu.VMEM((cap, sb, BLK), f32),
            pltpu.VMEM((cap, tb, BLK), f32),
            pltpu.VMEM((sb, BLK, LANES), f32),
            pltpu.VMEM((tb, BLK, LANES), f32),
            pltpu.VMEM((sb, 1, BLK), f32),
            pltpu.VMEM((tb, 1, BLK), f32),
            pltpu.VMEM((cap, 8, BLK), f32),
            pltpu.VMEM((cap, 8, BLK), f32),
            pltpu.VMEM((ITERS + 1, n_tgt, sb, BLK), f32),
            pltpu.VMEM((ITERS + 1, n_src, tb, BLK), f32),
            pltpu.VMEM((n_outer, tgt_own, width), f32),
            pltpu.VMEM((n_outer, tgt_own, width), f32),
            pltpu.VMEM((n_outer, tgt_own, width), f32),
            pltpu.VMEM((n_outer, tgt_own, width), f32),
            pltpu.VMEM((n_tgt, src_own, width), f32),
            pltpu.VMEM((n_tgt, src_own, width), f32),
            dma((ITERS + 1, n_tgt)),
            dma((ITERS + 1, n_tgt)),
            dma((ITERS + 1, n_src)),
            dma((ITERS + 1, n_src)),
            dma((n_outer,)),
            dma((n_outer,)),
            dma((n_outer,)),
            dma((n_outer,)),
            dma((n_tgt,)),
            dma((n_tgt,)),
        ],
        compiler_params=pltpu.CompilerParams(
            collective_id=0, has_side_effects=True, vmem_limit_bytes=50 * 1024 * 1024
        ),
    )(
        pair_blocks,
        pair_counts,
        slots,
        text_emb.reshape(sb, BLK, width),
        image_emb.reshape(tb, BLK, width),
        log_mass_src.reshape(sb, BLK),
        log_mass_tgt.reshape(tb, BLK),
    )


def solution(mesh):
    n_src, n_tgt = mesh.shape["src"], mesh.shape["tgt"]
    return jax.shard_map(
        functools.partial(local, n_src, n_tgt),
        mesh=mesh,
        in_specs=(
            P("src", None),
            P("tgt", None),
            P("src"),
            P("tgt"),
            P(("src", "tgt"), None),
            P(("src", "tgt")),
        ),
        out_specs=(P(("src", "tgt"), None), P(("tgt", "src"), None)),
        check_vma=False,
    )
```

```python
import functools

import jax
import jax.numpy as jnp
from jax import lax
from jax.experimental import pallas as pl
from jax.experimental.pallas import tpu as pltpu
from jax.sharding import PartitionSpec as P

BLK = 256
ITERS = 3
LANES = 128

inv_temp = 0.15
floor_value = -1e30
MESH = pl.DeviceIdType.MESH


def each(low, high, body):
    if high - low <= 8:
        for i in range(low, high):
            body(i)
    else:

        def step(i, carry):
            body(i)
            return carry

        lax.fori_loop(low, high, step, 0)


def looped(low, high, body, unroll=1):

    def step(i, carry):
        body(i)
        return carry

    lax.fori_loop(low, high, step, 0, unroll=unroll)


def partner(me, n, step):
    if n & (n - 1):
        return lax.rem(me + 1 + step, n)
    mask = n - 1 - step
    out = me * 0
    bit = 1
    while bit < n:
        out = out + ((me // bit + mask // bit) % 2) * bit
        bit *= 2
    return out


def kernel(
    n_src, n_tgt, inner,
    codes, slots, text_hbm, image_hbm, lines_src, lines_tgt,
    src_out, tgt_out,
    text, image, mass_src, mass_tgt,
    score, score_t, weight, weight_t, bias_src, bias_tgt,
    src_wide, tgt_wide, src_row, tgt_row, top, tot,
    src_parts, tgt_parts,
    pair_send, pair_got, outer_sum, outer_got, part_send, part_got,
    src_ss, src_rs, tgt_ss, tgt_rs,
    pair_ss, pair_rs, outer_ss, outer_rs, part_ss, part_rs, load_sem,
):
    cap = score.shape[0]
    sb, block, width = text.shape
    tb = image.shape[0]
    s = lax.axis_index("src")
    t = lax.axis_index("tgt")
    n_outer = n_src // inner
    outer, side = s // inner, s % inner
    mate = outer * inner + (inner - 1 - side)

    def greet(device):
        pl.semaphore_signal(barrier, inc=1, device_id=device, device_id_type=MESH)

    loads = [
        pltpu.make_async_copy(text_hbm, text, load_sem.at[0]),
        pltpu.make_async_copy(image_hbm, image, load_sem.at[1]),
    ]
    for load in loads:
        load.start()
    barrier = pltpu.get_barrier_semaphore()
    each(1, n_tgt, lambda d: greet((s, (t + d) % n_tgt)))
    each(1, n_src, lambda d: greet(((s + d) % n_src, t)))

    def src_of(k):
        return (codes[k] % (sb * tb)) // tb

    def tgt_of(k):
        return codes[k] % tb

    def make_bias(k):
        used = codes[k] < sb * tb
        rows = lax.broadcasted_iota(jnp.int32, (sb, block), 0)
        a = jnp.where(used, src_of(k), -1)
        bias_src[k] = jnp.where(rows == a, 0.0, floor_value)
        cols = lax.broadcasted_iota(jnp.int32, (tb, block), 0)
        b = jnp.where(used, tgt_of(k), -1)
        bias_tgt[k] = jnp.where(cols == b, 0.0, floor_value)

    def make_scores(k):
        rows, cols = text[src_of(k)], image[tgt_of(k)]
        nt = (((1,), (1,)), ((), ()))
        score[k] = lax.dot_general(rows, cols, nt, preferred_element_type=jnp.float32) * inv_temp
        score_t[k] = lax.dot_general(cols, rows, nt, preferred_element_type=jnp.float32) * inv_temp

    looped(0, cap, make_bias)
    for lines, mass in ((lines_src, mass_src), (lines_tgt, mass_tgt)):
        for c in range(mass.shape[0]):
            for h in range(block // LANES):
                line = c * (block // LANES) + h
                mass[c : c + 1, h * LANES : (h + 1) * LANES] = lines[line : line + 1, :]
    for load in loads:
        load.wait()
    looped(0, cap, make_scores, unroll=2)
    tgt_wide[...] = jnp.zeros_like(tgt_wide)
    pl.semaphore_wait(barrier, n_tgt - 1 + n_src - 1)

    def push(parts, step, me, n, device, ss, rs, d):
        return pltpu.make_async_remote_copy(
            src_ref=parts.at[step, me],
            dst_ref=parts.at[step, me],
            send_sem=ss.at[step, d],
            recv_sem=rs.at[step, me],
            device_id=device,
            device_id_type=MESH,
        )

    def arrival(parts, step, d, me, n, device, ss, rs):
        other = (me + d) % n
        return pltpu.make_async_remote_copy(
            src_ref=parts.at[step, other],
            dst_ref=parts.at[step, other],
            send_sem=ss.at[step, d],
            recv_sem=rs.at[step, other],
            device_id=device,
            device_id_type=MESH,
        )

    def src_group(d):
        return (s, (t + d) % n_tgt)

    def tgt_group(d):
        return ((s + d) % n_src, t)

    sides = {
        "src": (src_parts, t, n_tgt, src_group, src_ss, src_rs),
        "tgt": (tgt_parts, s, n_src, tgt_group, tgt_ss, tgt_rs),
    }

    def send_parts(which, step):
        parts, me, n, group, ss, rs = sides[which]
        each(1, n, lambda d: push(parts, step, me, n, group(d), ss, rs, d).start())

    def wait_parts(which, step):
        parts, me, n, group, ss, rs = sides[which]
        each(1, n, lambda d: arrival(parts, step, d, me, n, group(d), ss, rs).wait_recv())
        each(1, n, lambda d: push(parts, step, me, n, group(d), ss, rs, d).wait_send())

    def lse_pass(tiles, wide, cluster_of):

        def one(k):
            shift = wide[cluster_of(k)]
            for h in range(block // LANES):
                lanes = pl.ds(h * LANES, LANES)
                shifted = (tiles[k, :, lanes] + shift).reshape(block // 8, 8, LANES)
                peak = jnp.max(shifted, axis=0)
                top[k, :, lanes] = peak
                tot[k, :, lanes] = jnp.sum(jnp.exp(shifted - peak[None]), axis=0)

        looped(0, cap, one, unroll=4)

    def local_part(bias):
        peaks = top[...]
        peak = jnp.max(peaks, axis=1, keepdims=True)
        total = jnp.sum(tot[...] * jnp.exp(peaks - peak), axis=1, keepdims=True)
        masked = (peak + jnp.log(total)) + bias[...]
        highest = jnp.max(masked, axis=0)
        return highest + jnp.log(jnp.sum(jnp.exp(masked - highest[None]), axis=0))

    def merged(parts, step):
        every = parts[step]
        highest = jnp.max(every, axis=0)
        return highest + jnp.log(jnp.sum(jnp.exp(every - highest[None]), axis=0))

    def widen(value, wide):
        columns = value.T
        for c in range(value.shape[0]):
            wide[c] = jnp.broadcast_to(columns[:, c : c + 1], (block, LANES))

    def spread(value, row):
        for c in range(value.shape[0]):
            row[c] = value[c : c + 1, :]

    def iterate(step):
        lse_pass(score_t, tgt_wide, tgt_of)
        src_parts[step, t] = local_part(bias_src)
        send_parts("src", step)
        wait_parts("src", step)
        pot = mass_src[...] - merged(src_parts, step)
        widen(pot, src_wide)
        spread(pot, src_row)
        lse_pass(score, src_wide, src_of)
        tgt_parts[step, s] = local_part(bias_tgt)
        send_parts("tgt", step)
        wait_parts("tgt", step)
        pot = mass_tgt[...] - merged(tgt_parts, step)
        widen(pot, tgt_wide)
        spread(pot, tgt_row)

    looped(0, ITERS, iterate)

    def plan(k):
        a, b = src_of(k), tgt_of(k)
        for h in range(block // LANES):
            lanes = pl.ds(h * LANES, LANES)
            tile = score[k, :, lanes] + src_wide[a] + tgt_row[b, :, lanes]
            tile = jnp.exp(tile)
            weight[k, :, lanes] = tile.astype(jnp.bfloat16)
            top[k, :, lanes] = jnp.sum(tile.reshape(block // 8, 8, LANES), axis=0)
            tile = score_t[k, :, lanes] + src_row[a, :, lanes] + tgt_wide[b]
            tile = jnp.exp(tile)
            weight_t[k, :, lanes] = tile.astype(jnp.bfloat16)
            tot[k, :, lanes] = jnp.sum(tile.reshape(block // 8, 8, LANES), axis=0)

    looped(0, cap, plan, unroll=2)
    weight[cap] = jnp.zeros(weight.shape[1:], weight.dtype)
    weight_t[cap] = jnp.zeros(weight_t.shape[1:], weight_t.dtype)

    def mass_part(sums, bias):
        rows = jnp.sum(sums[...], axis=1, keepdims=True)
        return jnp.sum(jnp.where(bias[...] == 0.0, rows, 0.0), axis=0)

    src_parts[ITERS, t] = mass_part(tot, bias_src)
    tgt_parts[ITERS, s] = mass_part(top, bias_tgt)
    send_parts("tgt", ITERS)
    send_parts("src", ITERS)

    def unit_rows(n, clusters):
        own = clusters * block // n
        return own, min(own, block)

    tgt_own, tgt_unit = unit_rows(n_src, tb)
    src_own, src_unit = unit_rows(n_tgt, sb)

    def numer(start, unit, tiles, index, count_other, table):
        cluster, off = start // block, start % block
        picks = []
        for c in range(count_other):
            slot = slots[index(cluster, c)]
            if unit == block:
                picks.append(tiles[slot])
            else:
                picks.append(tiles[slot, pl.ds(pl.multiple_of(off, unit), unit), :])
        left = jnp.concatenate(picks, axis=1)
        right = table[...].reshape(count_other * block, width)
        return jnp.dot(left, right, preferred_element_type=jnp.float32)

    def tgt_numer(owner, out, where):
        for u in range(tgt_own // tgt_unit):
            start = owner * tgt_own + u * tgt_unit
            out[where, pl.ds(u * tgt_unit, tgt_unit), :] = numer(
                start, tgt_unit, weight_t, lambda j, a: a * tb + j, sb, text
            )

    def src_numer(owner, out, where):

        def unit(u):
            start = owner * src_own + u * src_unit
            rows = pl.ds(pl.multiple_of(u * src_unit, src_unit), src_unit)
            out[where, rows, :] = numer(start, src_unit, weight, lambda i, b: i * tb + b, tb, image)

        looped(0, src_own // src_unit, unit)

    halves = 2
    ahead = 3
    piece = tgt_own // halves
    last = (n_outer - 1) * halves

    def place(q):
        rows = pl.ds(pl.multiple_of((q % halves) * piece, piece), piece)
        return partner(outer, n_outer, q // halves), rows

    def pair_copy(q):
        z, rows = place(q)
        return pltpu.make_async_remote_copy(
            src_ref=pair_send.at[z, rows],
            dst_ref=pair_got.at[z, rows],
            send_sem=pair_ss.at[z, q % halves],
            recv_sem=pair_rs.at[z, q % halves],
            device_id=(mate, t),
            device_id_type=MESH,
        )

    def outer_copy(q, incoming=False):
        z, rows = place(q)
        slot = z if incoming else outer
        return pltpu.make_async_remote_copy(
            src_ref=outer_sum.at[z, rows],
            dst_ref=outer_got.at[slot, rows],
            send_sem=outer_ss.at[z, q % halves],
            recv_sem=outer_rs.at[slot, q % halves],
            device_id=(z * inner + side, t),
            device_id_type=MESH,
        )

    def part_copy(other, slot):
        return pltpu.make_async_remote_copy(
            src_ref=part_send.at[other],
            dst_ref=part_got.at[slot],
            send_sem=part_ss.at[other],
            recv_sem=part_rs.at[slot],
            device_id=(s, other),
            device_id_type=MESH,
        )

    def to_mate(step):
        z = partner(outer, n_outer, step)
        tgt_numer(z * inner + (inner - 1 - side), pair_send, z)
        for h in range(halves):
            q = step * halves + h
            pl.when(q < ahead)(lambda: pair_copy(q).start())

    def to_part(step):
        other = partner(t, n_tgt, step)
        src_numer(other, part_send, other)
        part_copy(other, t).start()

    def own_outer(step):
        z = partner(outer, n_outer, step)
        tgt_numer(z * inner + side, outer_sum, z)

    if inner == 2:
        looped(0, n_outer, to_mate)
    looped(0, n_tgt - 1, to_part)
    looped(0, n_outer, own_outer)

    def collect(q):
        if inner == 2:
            z, rows = place(q)
            pair_copy(q).wait_recv()
            pl.when(q + ahead < n_outer * halves)(lambda: pair_copy(q + ahead).start())
            outer_sum[z, rows] = outer_sum[z, rows] + pair_got[z, rows]

    def forward(q):
        collect(q)
        outer_copy(q).start()

    looped(0, last, forward)
    src_numer(t, part_send, t)
    looped(last, n_outer * halves, collect)

    wait_parts("src", ITERS)
    wait_parts("tgt", ITERS)
    widen(jnp.sum(src_parts[ITERS], axis=0), src_wide)
    widen(jnp.sum(tgt_parts[ITERS], axis=0), tgt_wide)

    def take_part(step):
        other = partner(t, n_tgt, step)
        part_copy(other, other).wait_recv()
        part_send[t] = part_send[t] + part_got[other]

    looped(0, n_tgt - 1, take_part)
    for u in range(src_own // src_unit):
        start = t * src_own + u * src_unit
        rows = pl.ds(u * src_unit, src_unit)
        off = pl.multiple_of(start % block, src_unit)
        mass = src_wide[start // block, pl.ds(off, src_unit), :]
        for c in range(width // LANES):
            lanes = pl.ds(c * LANES, LANES)
            src_out[rows, lanes] = part_send[t, rows, lanes] / mass

    def take_outer(q):
        z, rows = place(q)
        outer_copy(q, incoming=True).wait_recv()
        outer_sum[outer, rows] = outer_sum[outer, rows] + outer_got[z, rows]

    looped(0, last, take_outer)
    for u in range(tgt_own // tgt_unit):
        start = s * tgt_own + u * tgt_unit
        rows = pl.ds(u * tgt_unit, tgt_unit)
        off = pl.multiple_of(start % block, tgt_unit)
        mass = tgt_wide[start // block, pl.ds(off, tgt_unit), :]
        for c in range(width // LANES):
            lanes = pl.ds(c * LANES, LANES)
            tgt_out[rows, lanes] = outer_sum[outer, rows, lanes] / mass

    def sent_pair(q):
        pair_copy(q).wait_send()

    def sent_outer(q):
        outer_copy(q).wait_send()

    def sent_part(step):
        part_copy(partner(t, n_tgt, step), t).wait_send()

    if inner == 2:
        looped(0, n_outer * halves, sent_pair)
    looped(0, last, sent_outer)
    looped(0, n_tgt - 1, sent_part)


def local(n_src, n_tgt, text_emb, image_emb, log_mass_src, log_mass_tgt, pair_blocks, pair_counts):
    sb = text_emb.shape[0] // BLK
    tb = image_emb.shape[0] // BLK
    width = text_emb.shape[1]
    cap = pair_blocks.shape[0]
    inner = 2 if n_src % 2 == 0 else 1
    n_outer = n_src // inner
    tgt_own = tb * BLK // n_src
    src_own = sb * BLK // n_tgt

    slot_ids = jnp.arange(cap, dtype=jnp.int32)
    combo = pair_blocks[:, 0] * tb + pair_blocks[:, 1]
    codes = combo + jnp.where(slot_ids < pair_counts[0], 0, sb * tb)
    combos = jnp.arange(sb * tb, dtype=jnp.int32)
    slots = jnp.min(jnp.where(codes[None, :] == combos[:, None], slot_ids[None, :], cap), axis=1)

    f32, bf16 = jnp.float32, jnp.bfloat16
    dma = pltpu.SemaphoreType.DMA
    smem = pl.BlockSpec(memory_space=pltpu.SMEM)
    vmem = pl.BlockSpec(memory_space=pltpu.VMEM)
    return pl.pallas_call(
        functools.partial(kernel, n_src, n_tgt, inner),
        out_shape=(
            jax.ShapeDtypeStruct((src_own, width), f32),
            jax.ShapeDtypeStruct((tgt_own, width), f32),
        ),
        in_specs=[smem] * 2 + [pl.BlockSpec(memory_space=pltpu.HBM)] * 2 + [vmem] * 2,
        out_specs=(vmem, vmem),
        scratch_shapes=[
            pltpu.VMEM((sb, BLK, width), bf16),
            pltpu.VMEM((tb, BLK, width), bf16),
            pltpu.VMEM((sb, BLK), f32),
            pltpu.VMEM((tb, BLK), f32),
            pltpu.VMEM((cap, BLK, BLK), f32),
            pltpu.VMEM((cap, BLK, BLK), f32),
            pltpu.VMEM((cap + 1, BLK, BLK), bf16),
            pltpu.VMEM((cap + 1, BLK, BLK), bf16),
            pltpu.VMEM((cap, sb, BLK), f32),
            pltpu.VMEM((cap, tb, BLK), f32),
            pltpu.VMEM((sb, BLK, LANES), f32),
            pltpu.VMEM((tb, BLK, LANES), f32),
            pltpu.VMEM((sb, 1, BLK), f32),
            pltpu.VMEM((tb, 1, BLK), f32),
            pltpu.VMEM((cap, 8, BLK), f32),
            pltpu.VMEM((cap, 8, BLK), f32),
            pltpu.VMEM((ITERS + 1, n_tgt, sb, BLK), f32),
            pltpu.VMEM((ITERS + 1, n_src, tb, BLK), f32),
            pltpu.VMEM((n_outer, tgt_own, width), f32),
            pltpu.VMEM((n_outer, tgt_own, width), f32),
            pltpu.VMEM((n_outer, tgt_own, width), f32),
            pltpu.VMEM((n_outer, tgt_own, width), f32),
            pltpu.VMEM((n_tgt, src_own, width), f32),
            pltpu.VMEM((n_tgt, src_own, width), f32),
            dma((ITERS + 1, n_tgt)),
            dma((ITERS + 1, n_tgt)),
            dma((ITERS + 1, n_src)),
            dma((ITERS + 1, n_src)),
            dma((n_outer, 2)),
            dma((n_outer, 2)),
            dma((n_outer, 2)),
            dma((n_outer, 2)),
            dma((n_tgt,)),
            dma((n_tgt,)),
            dma((2,)),
        ],
        compiler_params=pltpu.CompilerParams(
            collective_id=0, has_side_effects=True, vmem_limit_bytes=50 * 1024 * 1024
        ),
    )(
        codes,
        slots,
        text_emb.reshape(sb, BLK, width),
        image_emb.reshape(tb, BLK, width),
        log_mass_src.reshape(-1, LANES),
        log_mass_tgt.reshape(-1, LANES),
    )


def solution(mesh):
    n_src, n_tgt = mesh.shape["src"], mesh.shape["tgt"]
    return jax.shard_map(
        functools.partial(local, n_src, n_tgt),
        mesh=mesh,
        in_specs=(
            P("src", None),
            P("tgt", None),
            P("src"),
            P("tgt"),
            P(("src", "tgt"), None),
            P(("src", "tgt")),
        ),
        out_specs=(P(("src", "tgt"), None), P(("tgt", "src"), None)),
        check_vma=False,
    )
```

```python
import functools

import jax
import jax.numpy as jnp
from jax import lax
from jax.experimental import pallas as pl
from jax.experimental.pallas import tpu as pltpu
from jax.sharding import PartitionSpec as P

BLK = 256
ITERS = 3
LANES = 128

inv_temp = 0.15
floor_value = -1e30
MESH = pl.DeviceIdType.MESH


def each(low, high, body):
    if high - low <= 8:
        for i in range(low, high):
            body(i)
    else:

        def step(i, carry):
            body(i)
            return carry

        lax.fori_loop(low, high, step, 0)


def looped(low, high, body, unroll=1):

    def step(i, carry):
        body(i)
        return carry

    lax.fori_loop(low, high, step, 0, unroll=unroll)


def partner(me, n, step):
    if n & (n - 1):
        return lax.rem(me + 1 + step, n)
    mask = n - 1 - step
    out = me * 0
    bit = 1
    while bit < n:
        out = out + ((me // bit + mask // bit) % 2) * bit
        bit *= 2
    return out


def kernel(
    n_src, n_tgt, inner,
    codes, slots, text_hbm, image_hbm, lines_src_hbm, lines_tgt_hbm,
    src_out, tgt_out,
    text, image, lines_src, lines_tgt, mass_src, mass_tgt,
    score, score_t, weight, weight_t, bias_src, bias_tgt,
    src_wide, tgt_wide, src_row, tgt_row, top, tot,
    src_parts, tgt_parts,
    pair_send, pair_got, outer_sum, outer_got, part_send, part_got,
    src_ss, src_rs, tgt_ss, tgt_rs,
    pair_ss, pair_rs, outer_ss, outer_rs, part_ss, part_rs, load_sem,
):
    cap = score.shape[0]
    sb, block, width = text.shape
    tb = image.shape[0]
    s = lax.axis_index("src")
    t = lax.axis_index("tgt")
    n_outer = n_src // inner
    outer, side = s // inner, s % inner
    mate = outer * inner + (inner - 1 - side)

    def greet(device):
        pl.semaphore_signal(barrier, inc=1, device_id=device, device_id_type=MESH)

    loads = [
        pltpu.make_async_copy(text_hbm, text, load_sem.at[0]),
        pltpu.make_async_copy(image_hbm, image, load_sem.at[1]),
        pltpu.make_async_copy(lines_src_hbm, lines_src, load_sem.at[2]),
        pltpu.make_async_copy(lines_tgt_hbm, lines_tgt, load_sem.at[3]),
    ]
    for load in loads:
        load.start()
    barrier = pltpu.get_barrier_semaphore()
    each(1, n_tgt, lambda d: greet((s, (t + d) % n_tgt)))
    each(1, n_src, lambda d: greet(((s + d) % n_src, t)))

    def src_of(k):
        return (codes[k] % (sb * tb)) // tb

    def tgt_of(k):
        return codes[k] % tb

    def make_bias(k):
        used = codes[k] < sb * tb
        rows = lax.broadcasted_iota(jnp.int32, (sb, block), 0)
        a = jnp.where(used, src_of(k), -1)
        bias_src[k] = jnp.where(rows == a, 0.0, floor_value)
        cols = lax.broadcasted_iota(jnp.int32, (tb, block), 0)
        b = jnp.where(used, tgt_of(k), -1)
        bias_tgt[k] = jnp.where(cols == b, 0.0, floor_value)

    def add_up(k, h, shifted):
        lanes = pl.ds(h * LANES, LANES)
        shifted = shifted.reshape(block // 8, 8, LANES)
        peak = jnp.max(shifted, axis=0)
        top[k, :, lanes] = peak
        tot[k, :, lanes] = jnp.sum(jnp.exp(shifted - peak[None]), axis=0)

    def make_scores(k):
        rows, cols = text[src_of(k)], image[tgt_of(k)]
        nt = (((1,), (1,)), ((), ()))
        score[k] = lax.dot_general(rows, cols, nt, preferred_element_type=jnp.float32) * inv_temp
        tile = lax.dot_general(cols, rows, nt, preferred_element_type=jnp.float32) * inv_temp
        score_t[k] = tile
        for h in range(block // LANES):
            add_up(k, h, tile[:, h * LANES : (h + 1) * LANES])

    looped(0, cap, make_bias)
    for load in loads:
        load.wait()
    for lines, mass in ((lines_src, mass_src), (lines_tgt, mass_tgt)):
        for c in range(mass.shape[0]):
            for h in range(block // LANES):
                line = c * (block // LANES) + h
                mass[c : c + 1, h * LANES : (h + 1) * LANES] = lines[line : line + 1, :]
    looped(0, cap, make_scores, unroll=2)
    pl.semaphore_wait(barrier, n_tgt - 1 + n_src - 1)

    def push(parts, step, me, n, device, ss, rs, d):
        return pltpu.make_async_remote_copy(
            src_ref=parts.at[step, me],
            dst_ref=parts.at[step, me],
            send_sem=ss.at[step, d],
            recv_sem=rs.at[step, me],
            device_id=device,
            device_id_type=MESH,
        )

    def arrival(parts, step, d, me, n, device, ss, rs):
        other = (me + d) % n
        return pltpu.make_async_remote_copy(
            src_ref=parts.at[step, other],
            dst_ref=parts.at[step, other],
            send_sem=ss.at[step, d],
            recv_sem=rs.at[step, other],
            device_id=device,
            device_id_type=MESH,
        )

    def src_group(d):
        return (s, (t + d) % n_tgt)

    def tgt_group(d):
        return ((s + d) % n_src, t)

    sides = {
        "src": (src_parts, t, n_tgt, src_group, src_ss, src_rs),
        "tgt": (tgt_parts, s, n_src, tgt_group, tgt_ss, tgt_rs),
    }

    def send_parts(which, step):
        parts, me, n, group, ss, rs = sides[which]
        each(1, n, lambda d: push(parts, step, me, n, group(d), ss, rs, d).start())

    def wait_parts(which, step):
        parts, me, n, group, ss, rs = sides[which]
        each(1, n, lambda d: arrival(parts, step, d, me, n, group(d), ss, rs).wait_recv())
        each(1, n, lambda d: push(parts, step, me, n, group(d), ss, rs, d).wait_send())

    def lse_pass(tiles, wide, cluster_of):

        def one(k):
            shift = wide[cluster_of(k)]
            for h in range(block // LANES):
                lanes = pl.ds(h * LANES, LANES)
                add_up(k, h, tiles[k, :, lanes] + shift)

        looped(0, cap, one, unroll=4)

    def local_part(bias):
        peaks = top[...]
        peak = jnp.max(peaks, axis=1, keepdims=True)
        total = jnp.sum(tot[...] * jnp.exp(peaks - peak), axis=1, keepdims=True)
        masked = (peak + jnp.log(total)) + bias[...]
        highest = jnp.max(masked, axis=0)
        return highest + jnp.log(jnp.sum(jnp.exp(masked - highest[None]), axis=0))

    def merged(parts, step):
        every = parts[step]
        highest = jnp.max(every, axis=0)
        return highest + jnp.log(jnp.sum(jnp.exp(every - highest[None]), axis=0))

    def widen(value, wide):
        columns = value.T
        for c in range(value.shape[0]):
            wide[c] = jnp.broadcast_to(columns[:, c : c + 1], (block, LANES))

    def spread(value, row):
        for c in range(value.shape[0]):
            row[c] = value[c : c + 1, :]

    def iterate(step):
        pl.when(step > 0)(lambda: lse_pass(score_t, tgt_wide, tgt_of))
        src_parts[step, t] = local_part(bias_src)
        send_parts("src", step)
        wait_parts("src", step)
        pot = mass_src[...] - merged(src_parts, step)
        widen(pot, src_wide)
        spread(pot, src_row)
        lse_pass(score, src_wide, src_of)
        tgt_parts[step, s] = local_part(bias_tgt)
        send_parts("tgt", step)
        wait_parts("tgt", step)
        pot = mass_tgt[...] - merged(tgt_parts, step)
        widen(pot, tgt_wide)
        spread(pot, tgt_row)

    looped(0, ITERS, iterate)

    def plan_tgt(k):
        a, b = src_of(k), tgt_of(k)
        for h in range(block // LANES):
            lanes = pl.ds(h * LANES, LANES)
            tile = jnp.exp(score_t[k, :, lanes] + src_row[a, :, lanes] + tgt_wide[b])
            weight_t[k, :, lanes] = tile.astype(jnp.bfloat16)
            tot[k, :, lanes] = jnp.sum(tile.reshape(block // 8, 8, LANES), axis=0)

    def plan_src(k):
        a, b = src_of(k), tgt_of(k)
        for h in range(block // LANES):
            lanes = pl.ds(h * LANES, LANES)
            tile = jnp.exp(score[k, :, lanes] + src_wide[a] + tgt_row[b, :, lanes])
            weight[k, :, lanes] = tile.astype(jnp.bfloat16)
            top[k, :, lanes] = jnp.sum(tile.reshape(block // 8, 8, LANES), axis=0)

    def mass_part(sums, bias):
        rows = jnp.sum(sums[...], axis=1, keepdims=True)
        return jnp.sum(jnp.where(bias[...] == 0.0, rows, 0.0), axis=0)

    def unit_rows(n, clusters):
        own = clusters * block // n
        return own, min(own, block)

    tgt_own, tgt_unit = unit_rows(n_src, tb)
    src_own, src_unit = unit_rows(n_tgt, sb)

    def numer(start, unit, tiles, index, count_other, table):
        cluster, off = start // block, start % block
        picks = []
        for c in range(count_other):
            slot = slots[index(cluster, c)]
            if unit == block:
                picks.append(tiles[slot])
            else:
                picks.append(tiles[slot, pl.ds(pl.multiple_of(off, unit), unit), :])
        left = jnp.concatenate(picks, axis=1)
        right = table[...].reshape(count_other * block, width)
        return jnp.dot(left, right, preferred_element_type=jnp.float32)

    def tgt_numer(owner, out, where):
        for u in range(tgt_own // tgt_unit):
            start = owner * tgt_own + u * tgt_unit
            out[where, pl.ds(u * tgt_unit, tgt_unit), :] = numer(
                start, tgt_unit, weight_t, lambda j, a: a * tb + j, sb, text
            )

    def src_numer(owner, out, where):

        def unit(u):
            start = owner * src_own + u * src_unit
            rows = pl.ds(pl.multiple_of(u * src_unit, src_unit), src_unit)
            out[where, rows, :] = numer(start, src_unit, weight, lambda i, b: i * tb + b, tb, image)

        looped(0, src_own // src_unit, unit)

    halves = 2
    ahead = 3
    piece = tgt_own // halves
    last = (n_outer - 1) * halves

    def place(q):
        rows = pl.ds(pl.multiple_of((q % halves) * piece, piece), piece)
        return partner(outer, n_outer, q // halves), rows

    def pair_copy(q):
        z, rows = place(q)
        return pltpu.make_async_remote_copy(
            src_ref=pair_send.at[z, rows],
            dst_ref=pair_got.at[z, rows],
            send_sem=pair_ss.at[z, q % halves],
            recv_sem=pair_rs.at[z, q % halves],
            device_id=(mate, t),
            device_id_type=MESH,
        )

    def outer_copy(q, incoming=False):
        z, rows = place(q)
        slot = z if incoming else outer
        return pltpu.make_async_remote_copy(
            src_ref=outer_sum.at[z, rows],
            dst_ref=outer_got.at[slot, rows],
            send_sem=outer_ss.at[z, q % halves],
            recv_sem=outer_rs.at[slot, q % halves],
            device_id=(z * inner + side, t),
            device_id_type=MESH,
        )

    def part_copy(other, slot):
        return pltpu.make_async_remote_copy(
            src_ref=part_send.at[other],
            dst_ref=part_got.at[slot],
            send_sem=part_ss.at[other],
            recv_sem=part_rs.at[slot],
            device_id=(s, other),
            device_id_type=MESH,
        )

    def to_mate(step):
        z = partner(outer, n_outer, step)
        tgt_numer(z * inner + (inner - 1 - side), pair_send, z)
        for h in range(halves):
            q = step * halves + h
            pl.when(q < ahead)(lambda: pair_copy(q).start())

    def to_part(step):
        other = partner(t, n_tgt, step)
        src_numer(other, part_send, other)
        part_copy(other, t).start()

    def own_outer(step):
        z = partner(outer, n_outer, step)
        tgt_numer(z * inner + side, outer_sum, z)

    looped(0, cap, plan_tgt, unroll=2)
    weight_t[cap] = jnp.zeros(weight_t.shape[1:], weight_t.dtype)
    if inner == 2:
        looped(0, n_outer, to_mate)
    looped(0, cap, plan_src, unroll=2)
    weight[cap] = jnp.zeros(weight.shape[1:], weight.dtype)
    src_parts[ITERS, t] = mass_part(tot, bias_src)
    tgt_parts[ITERS, s] = mass_part(top, bias_tgt)
    send_parts("tgt", ITERS)
    send_parts("src", ITERS)
    looped(0, n_tgt - 1, to_part)
    looped(0, n_outer, own_outer)

    def collect(q):
        if inner == 2:
            z, rows = place(q)
            pair_copy(q).wait_recv()
            pl.when(q + ahead < n_outer * halves)(lambda: pair_copy(q + ahead).start())
            outer_sum[z, rows] = outer_sum[z, rows] + pair_got[z, rows]

    def forward(q):
        collect(q)
        outer_copy(q).start()

    looped(0, last, forward)
    src_numer(t, part_send, t)
    looped(last, n_outer * halves, collect)

    wait_parts("src", ITERS)
    wait_parts("tgt", ITERS)
    widen(jnp.sum(src_parts[ITERS], axis=0), src_wide)
    widen(jnp.sum(tgt_parts[ITERS], axis=0), tgt_wide)

    def take_part(step):
        other = partner(t, n_tgt, step)
        part_copy(other, other).wait_recv()
        part_send[t] = part_send[t] + part_got[other]

    looped(0, n_tgt - 1, take_part)
    for u in range(src_own // src_unit):
        start = t * src_own + u * src_unit
        rows = pl.ds(u * src_unit, src_unit)
        off = pl.multiple_of(start % block, src_unit)
        mass = src_wide[start // block, pl.ds(off, src_unit), :]
        for c in range(width // LANES):
            lanes = pl.ds(c * LANES, LANES)
            src_out[rows, lanes] = part_send[t, rows, lanes] / mass

    def take_outer(q):
        z, rows = place(q)
        outer_copy(q, incoming=True).wait_recv()
        outer_sum[outer, rows] = outer_sum[outer, rows] + outer_got[z, rows]

    looped(0, last, take_outer)
    for u in range(tgt_own // tgt_unit):
        start = s * tgt_own + u * tgt_unit
        rows = pl.ds(u * tgt_unit, tgt_unit)
        off = pl.multiple_of(start % block, tgt_unit)
        mass = tgt_wide[start // block, pl.ds(off, tgt_unit), :]
        for c in range(width // LANES):
            lanes = pl.ds(c * LANES, LANES)
            tgt_out[rows, lanes] = outer_sum[outer, rows, lanes] / mass

    def sent_pair(q):
        pair_copy(q).wait_send()

    def sent_outer(q):
        outer_copy(q).wait_send()

    def sent_part(step):
        part_copy(partner(t, n_tgt, step), t).wait_send()

    if inner == 2:
        looped(0, n_outer * halves, sent_pair)
    looped(0, last, sent_outer)
    looped(0, n_tgt - 1, sent_part)


def local(n_src, n_tgt, text_emb, image_emb, log_mass_src, log_mass_tgt, pair_blocks, pair_counts):
    sb = text_emb.shape[0] // BLK
    tb = image_emb.shape[0] // BLK
    width = text_emb.shape[1]
    cap = pair_blocks.shape[0]
    inner = 2 if n_src % 2 == 0 else 1
    n_outer = n_src // inner
    tgt_own = tb * BLK // n_src
    src_own = sb * BLK // n_tgt

    slot_ids = jnp.arange(cap, dtype=jnp.int32)
    combo = pair_blocks[:, 0] * tb + pair_blocks[:, 1]
    codes = combo + jnp.where(slot_ids < pair_counts[0], 0, sb * tb)
    combos = jnp.arange(sb * tb, dtype=jnp.int32)
    slots = jnp.min(jnp.where(codes[None, :] == combos[:, None], slot_ids[None, :], cap), axis=1)

    f32, bf16 = jnp.float32, jnp.bfloat16
    dma = pltpu.SemaphoreType.DMA
    smem = pl.BlockSpec(memory_space=pltpu.SMEM)
    vmem = pl.BlockSpec(memory_space=pltpu.VMEM)
    return pl.pallas_call(
        functools.partial(kernel, n_src, n_tgt, inner),
        out_shape=(
            jax.ShapeDtypeStruct((src_own, width), f32),
            jax.ShapeDtypeStruct((tgt_own, width), f32),
        ),
        in_specs=[smem] * 2 + [pl.BlockSpec(memory_space=pltpu.HBM)] * 4,
        out_specs=(vmem, vmem),
        scratch_shapes=[
            pltpu.VMEM((sb, BLK, width), bf16),
            pltpu.VMEM((tb, BLK, width), bf16),
            pltpu.VMEM((sb * BLK // LANES, LANES), f32),
            pltpu.VMEM((tb * BLK // LANES, LANES), f32),
            pltpu.VMEM((sb, BLK), f32),
            pltpu.VMEM((tb, BLK), f32),
            pltpu.VMEM((cap, BLK, BLK), f32),
            pltpu.VMEM((cap, BLK, BLK), f32),
            pltpu.VMEM((cap + 1, BLK, BLK), bf16),
            pltpu.VMEM((cap + 1, BLK, BLK), bf16),
            pltpu.VMEM((cap, sb, BLK), f32),
            pltpu.VMEM((cap, tb, BLK), f32),
            pltpu.VMEM((sb, BLK, LANES), f32),
            pltpu.VMEM((tb, BLK, LANES), f32),
            pltpu.VMEM((sb, 1, BLK), f32),
            pltpu.VMEM((tb, 1, BLK), f32),
            pltpu.VMEM((cap, 8, BLK), f32),
            pltpu.VMEM((cap, 8, BLK), f32),
            pltpu.VMEM((ITERS + 1, n_tgt, sb, BLK), f32),
            pltpu.VMEM((ITERS + 1, n_src, tb, BLK), f32),
            pltpu.VMEM((n_outer, tgt_own, width), f32),
            pltpu.VMEM((n_outer, tgt_own, width), f32),
            pltpu.VMEM((n_outer, tgt_own, width), f32),
            pltpu.VMEM((n_outer, tgt_own, width), f32),
            pltpu.VMEM((n_tgt, src_own, width), f32),
            pltpu.VMEM((n_tgt, src_own, width), f32),
            dma((ITERS + 1, n_tgt)),
            dma((ITERS + 1, n_tgt)),
            dma((ITERS + 1, n_src)),
            dma((ITERS + 1, n_src)),
            dma((n_outer, 2)),
            dma((n_outer, 2)),
            dma((n_outer, 2)),
            dma((n_outer, 2)),
            dma((n_tgt,)),
            dma((n_tgt,)),
            dma((4,)),
        ],
        compiler_params=pltpu.CompilerParams(
            collective_id=0, has_side_effects=True, vmem_limit_bytes=56 * 1024 * 1024
        ),
    )(
        codes,
        slots,
        text_emb.reshape(sb, BLK, width),
        image_emb.reshape(tb, BLK, width),
        log_mass_src.reshape(-1, LANES),
        log_mass_tgt.reshape(-1, LANES),
    )


def solution(mesh):
    n_src, n_tgt = mesh.shape["src"], mesh.shape["tgt"]
    return jax.shard_map(
        functools.partial(local, n_src, n_tgt),
        mesh=mesh,
        in_specs=(
            P("src", None),
            P("tgt", None),
            P("src"),
            P("tgt"),
            P(("src", "tgt"), None),
            P(("src", "tgt")),
        ),
        out_specs=(P(("src", "tgt"), None), P(("tgt", "src"), None)),
        check_vma=False,
    )
```

```python
import functools

import jax
import jax.numpy as jnp
from jax import lax
from jax.experimental import pallas as pl
from jax.experimental.pallas import tpu as pltpu
from jax.sharding import PartitionSpec as P

BLK = 256
ITERS = 3
LANES = 128

inv_temp = 0.15
floor_value = -1e30
MESH = pl.DeviceIdType.MESH


def each(low, high, body):
    if high - low <= 8:
        for i in range(low, high):
            body(i)
    else:

        def step(i, carry):
            body(i)
            return carry

        lax.fori_loop(low, high, step, 0)


def looped(low, high, body, unroll=1):

    def step(i, carry):
        body(i)
        return carry

    lax.fori_loop(low, high, step, 0, unroll=unroll)


def partner(me, n, step):
    if n & (n - 1):
        return lax.rem(me + 1 + step, n)
    mask = n - 1 - step
    out = me * 0
    bit = 1
    while bit < n:
        out = out + ((me // bit + mask // bit) % 2) * bit
        bit *= 2
    return out


def kernel(
    n_src, n_tgt, inner,
    codes, slots, text_hbm, image_hbm, lines_src_hbm, lines_tgt_hbm,
    src_out, tgt_out,
    text, image, lines_src, lines_tgt, mass_src, mass_tgt,
    score, score_t, weight, weight_t, bias_src, bias_tgt,
    src_wide, tgt_wide, src_row, tgt_row, top, tot,
    src_parts, tgt_parts,
    pair_send, pair_got, outer_sum, outer_got, part_send, part_got,
    src_ss, src_rs, tgt_ss, tgt_rs,
    pair_ss, pair_rs, outer_ss, outer_rs, part_ss, part_rs, load_sem,
):
    cap = score.shape[0]
    sb, block, width = text.shape
    tb = image.shape[0]
    s = lax.axis_index("src")
    t = lax.axis_index("tgt")
    n_outer = n_src // inner
    outer, side = s // inner, s % inner
    mate = outer * inner + (inner - 1 - side)

    def greet(device):
        pl.semaphore_signal(barrier, inc=1, device_id=device, device_id_type=MESH)

    loads = [
        pltpu.make_async_copy(text_hbm, text, load_sem.at[0]),
        pltpu.make_async_copy(image_hbm, image, load_sem.at[1]),
        pltpu.make_async_copy(lines_src_hbm, lines_src, load_sem.at[2]),
        pltpu.make_async_copy(lines_tgt_hbm, lines_tgt, load_sem.at[3]),
    ]
    for load in loads:
        load.start()
    barrier = pltpu.get_barrier_semaphore()
    each(1, n_tgt, lambda d: greet((s, (t + d) % n_tgt)))
    each(1, n_src, lambda d: greet(((s + d) % n_src, t)))

    def src_of(k):
        return (codes[k] % (sb * tb)) // tb

    def tgt_of(k):
        return codes[k] % tb

    def make_bias(k):
        used = codes[k] < sb * tb
        rows = lax.broadcasted_iota(jnp.int32, (sb, block), 0)
        a = jnp.where(used, src_of(k), -1)
        bias_src[k] = jnp.where(rows == a, 0.0, floor_value)
        cols = lax.broadcasted_iota(jnp.int32, (tb, block), 0)
        b = jnp.where(used, tgt_of(k), -1)
        bias_tgt[k] = jnp.where(cols == b, 0.0, floor_value)

    def add_up(k, h, shifted):
        lanes = pl.ds(h * LANES, LANES)
        shifted = shifted.reshape(block // 8, 8, LANES)
        peak = jnp.max(shifted, axis=0)
        top[k, :, lanes] = peak
        tot[k, :, lanes] = jnp.sum(jnp.exp(shifted - peak[None]), axis=0)

    def make_scores(k):
        rows, cols = text[src_of(k)], image[tgt_of(k)]
        nt = (((1,), (1,)), ((), ()))
        score[k] = lax.dot_general(rows, cols, nt, preferred_element_type=jnp.float32) * inv_temp
        tile = lax.dot_general(cols, rows, nt, preferred_element_type=jnp.float32) * inv_temp
        score_t[k] = tile
        for h in range(block // LANES):
            add_up(k, h, tile[:, h * LANES : (h + 1) * LANES])

    looped(0, cap, make_bias)
    for load in loads:
        load.wait()
    for lines, mass in ((lines_src, mass_src), (lines_tgt, mass_tgt)):
        for c in range(mass.shape[0]):
            for h in range(block // LANES):
                line = c * (block // LANES) + h
                mass[c : c + 1, h * LANES : (h + 1) * LANES] = lines[line : line + 1, :]
    looped(0, cap, make_scores, unroll=2)
    pl.semaphore_wait(barrier, n_tgt - 1 + n_src - 1)

    def push(parts, step, me, n, device, ss, rs, d):
        return pltpu.make_async_remote_copy(
            src_ref=parts.at[step, me],
            dst_ref=parts.at[step, me],
            send_sem=ss.at[step, d],
            recv_sem=rs.at[step, me],
            device_id=device,
            device_id_type=MESH,
        )

    def arrival(parts, step, d, me, n, device, ss, rs):
        other = (me + d) % n
        return pltpu.make_async_remote_copy(
            src_ref=parts.at[step, other],
            dst_ref=parts.at[step, other],
            send_sem=ss.at[step, d],
            recv_sem=rs.at[step, other],
            device_id=device,
            device_id_type=MESH,
        )

    def src_group(d):
        return (s, (t + d) % n_tgt)

    def tgt_group(d):
        return ((s + d) % n_src, t)

    sides = {
        "src": (src_parts, t, n_tgt, src_group, src_ss, src_rs),
        "tgt": (tgt_parts, s, n_src, tgt_group, tgt_ss, tgt_rs),
    }

    def send_parts(which, step):
        parts, me, n, group, ss, rs = sides[which]
        each(1, n, lambda d: push(parts, step, me, n, group(d), ss, rs, d).start())

    def wait_parts(which, step):
        parts, me, n, group, ss, rs = sides[which]
        each(1, n, lambda d: arrival(parts, step, d, me, n, group(d), ss, rs).wait_recv())
        each(1, n, lambda d: push(parts, step, me, n, group(d), ss, rs, d).wait_send())

    def lse_pass(tiles, wide, cluster_of):

        def one(k):
            shift = wide[cluster_of(k)]
            for h in range(block // LANES):
                lanes = pl.ds(h * LANES, LANES)
                add_up(k, h, tiles[k, :, lanes] + shift)

        looped(0, cap, one, unroll=4)

    def local_part(bias):
        peaks = top[...]
        peak = jnp.max(peaks, axis=1, keepdims=True)
        total = jnp.sum(tot[...] * jnp.exp(peaks - peak), axis=1, keepdims=True)
        masked = (peak + jnp.log(total)) + bias[...]
        highest = jnp.max(masked, axis=0)
        return highest + jnp.log(jnp.sum(jnp.exp(masked - highest[None]), axis=0))

    def merged(parts, step):
        every = parts[step]
        highest = jnp.max(every, axis=0)
        return highest + jnp.log(jnp.sum(jnp.exp(every - highest[None]), axis=0))

    def widen(value, wide):
        columns = value.T
        for c in range(value.shape[0]):
            wide[c] = jnp.broadcast_to(columns[:, c : c + 1], (block, LANES))

    def spread(value, row):
        for c in range(value.shape[0]):
            row[c] = value[c : c + 1, :]

    def iterate(step):
        pl.when(step > 0)(lambda: lse_pass(score_t, tgt_wide, tgt_of))
        src_parts[step, t] = local_part(bias_src)
        send_parts("src", step)
        wait_parts("src", step)
        pot = mass_src[...] - merged(src_parts, step)
        widen(pot, src_wide)
        spread(pot, src_row)
        lse_pass(score, src_wide, src_of)
        tgt_parts[step, s] = local_part(bias_tgt)
        send_parts("tgt", step)
        wait_parts("tgt", step)
        pot = mass_tgt[...] - merged(tgt_parts, step)
        widen(pot, tgt_wide)
        spread(pot, tgt_row)

    looped(0, ITERS, iterate)

    def plan_tgt(k):
        a, b = src_of(k), tgt_of(k)
        for h in range(block // LANES):
            lanes = pl.ds(h * LANES, LANES)
            tile = jnp.exp(score_t[k, :, lanes] + src_row[a, :, lanes] + tgt_wide[b])
            weight_t[k, :, lanes] = tile.astype(jnp.bfloat16)
            tot[k, :, lanes] = jnp.sum(tile.reshape(block // 8, 8, LANES), axis=0)

    def plan_src(k):
        a, b = src_of(k), tgt_of(k)
        for h in range(block // LANES):
            lanes = pl.ds(h * LANES, LANES)
            tile = jnp.exp(score[k, :, lanes] + src_wide[a] + tgt_row[b, :, lanes])
            weight[k, :, lanes] = tile.astype(jnp.bfloat16)
            top[k, :, lanes] = jnp.sum(tile.reshape(block // 8, 8, LANES), axis=0)

    def mass_part(sums, bias):
        rows = jnp.sum(sums[...], axis=1, keepdims=True)
        return jnp.sum(jnp.where(bias[...] == 0.0, rows, 0.0), axis=0)

    def unit_rows(n, clusters):
        own = clusters * block // n
        return own, min(own, block)

    tgt_own, tgt_unit = unit_rows(n_src, tb)
    src_own, src_unit = unit_rows(n_tgt, sb)

    def numer(start, unit, tiles, index, count_other, table):
        cluster, off = start // block, start % block
        picks = []
        for c in range(count_other):
            slot = slots[index(cluster, c)]
            if unit == block:
                picks.append(tiles[slot])
            else:
                picks.append(tiles[slot, pl.ds(pl.multiple_of(off, unit), unit), :])
        left = jnp.concatenate(picks, axis=1)
        right = table[...].reshape(count_other * block, width)
        return jnp.dot(left, right, preferred_element_type=jnp.float32)

    def tgt_numer(owner, out, where):
        for u in range(tgt_own // tgt_unit):
            start = owner * tgt_own + u * tgt_unit
            out[where, pl.ds(u * tgt_unit, tgt_unit), :] = numer(
                start, tgt_unit, weight_t, lambda j, a: a * tb + j, sb, text
            )

    def src_numer(owner, out, where):

        def unit(u):
            start = owner * src_own + u * src_unit
            rows = pl.ds(pl.multiple_of(u * src_unit, src_unit), src_unit)
            out[where, rows, :] = numer(start, src_unit, weight, lambda i, b: i * tb + b, tb, image)

        looped(0, src_own // src_unit, unit)

    halves = 2
    ahead = 3
    piece = tgt_own // halves
    last = (n_outer - 1) * halves

    def place(q):
        rows = pl.ds(pl.multiple_of((q % halves) * piece, piece), piece)
        return partner(outer, n_outer, q // halves), rows

    def pair_copy(q):
        z, rows = place(q)
        return pltpu.make_async_remote_copy(
            src_ref=pair_send.at[z, rows],
            dst_ref=pair_got.at[z, rows],
            send_sem=pair_ss.at[z, q % halves],
            recv_sem=pair_rs.at[z, q % halves],
            device_id=(mate, t),
            device_id_type=MESH,
        )

    def outer_copy(q, incoming=False):
        z, rows = place(q)
        slot = z if incoming else outer
        return pltpu.make_async_remote_copy(
            src_ref=outer_sum.at[z, rows],
            dst_ref=outer_got.at[slot, rows],
            send_sem=outer_ss.at[z, q % halves],
            recv_sem=outer_rs.at[slot, q % halves],
            device_id=(z * inner + side, t),
            device_id_type=MESH,
        )

    def part_copy(other, slot):
        return pltpu.make_async_remote_copy(
            src_ref=part_send.at[other],
            dst_ref=part_got.at[slot],
            send_sem=part_ss.at[other],
            recv_sem=part_rs.at[slot],
            device_id=(s, other),
            device_id_type=MESH,
        )

    def to_mate(step):
        z = partner(outer, n_outer, step)
        tgt_numer(z * inner + (inner - 1 - side), pair_send, z)
        for h in range(halves):
            q = step * halves + h
            pl.when(q < ahead)(lambda: pair_copy(q).start())

    def to_part(step):
        other = partner(t, n_tgt, step)
        src_numer(other, part_send, other)
        part_copy(other, t).start()

    def own_outer(step):
        z = partner(outer, n_outer, step)
        tgt_numer(z * inner + side, outer_sum, z)

    looped(0, cap, plan_tgt, unroll=2)
    weight_t[cap] = jnp.zeros(weight_t.shape[1:], weight_t.dtype)
    if inner == 2:
        looped(0, n_outer, to_mate)
    looped(0, cap, plan_src, unroll=2)
    weight[cap] = jnp.zeros(weight.shape[1:], weight.dtype)
    src_parts[ITERS, t] = mass_part(tot, bias_src)
    tgt_parts[ITERS, s] = mass_part(top, bias_tgt)
    send_parts("tgt", ITERS)
    send_parts("src", ITERS)
    looped(0, n_tgt - 1, to_part)
    looped(0, n_outer, own_outer)

    def collect(q):
        if inner == 2:
            z, rows = place(q)
            pair_copy(q).wait_recv()
            pl.when(q + ahead < n_outer * halves)(lambda: pair_copy(q + ahead).start())
            outer_sum[z, rows] = outer_sum[z, rows] + pair_got[z, rows]

    def forward(q):
        collect(q)
        outer_copy(q).start()

    looped(0, last, forward)
    src_numer(t, part_send, t)
    looped(last, n_outer * halves, collect)

    wait_parts("src", ITERS)
    wait_parts("tgt", ITERS)
    widen(jnp.sum(src_parts[ITERS], axis=0), src_wide)
    widen(jnp.sum(tgt_parts[ITERS], axis=0), tgt_wide)

    def take_part(step):
        other = partner(t, n_tgt, step)
        part_copy(other, other).wait_recv()
        part_send[t] = part_send[t] + part_got[other]

    looped(0, n_tgt - 1, take_part)
    for u in range(src_own // src_unit):
        start = t * src_own + u * src_unit
        rows = pl.ds(u * src_unit, src_unit)
        off = pl.multiple_of(start % block, src_unit)
        mass = src_wide[start // block, pl.ds(off, src_unit), :]
        for c in range(width // LANES):
            lanes = pl.ds(c * LANES, LANES)
            src_out[rows, lanes] = part_send[t, rows, lanes] / mass

    def take_outer(q):
        z, rows = place(q)
        outer_copy(q, incoming=True).wait_recv()
        outer_sum[outer, rows] = outer_sum[outer, rows] + outer_got[z, rows]

    looped(0, last, take_outer)
    for u in range(tgt_own // tgt_unit):
        start = s * tgt_own + u * tgt_unit
        rows = pl.ds(u * tgt_unit, tgt_unit)
        off = pl.multiple_of(start % block, tgt_unit)
        mass = tgt_wide[start // block, pl.ds(off, tgt_unit), :]
        for c in range(width // LANES):
            lanes = pl.ds(c * LANES, LANES)
            tgt_out[rows, lanes] = outer_sum[outer, rows, lanes] / mass

    def sent_pair(q):
        pair_copy(q).wait_send()

    def sent_outer(q):
        outer_copy(q).wait_send()

    def sent_part(step):
        part_copy(partner(t, n_tgt, step), t).wait_send()

    if inner == 2:
        looped(0, n_outer * halves, sent_pair)
    looped(0, last, sent_outer)
    looped(0, n_tgt - 1, sent_part)


def local(n_src, n_tgt, text_emb, image_emb, log_mass_src, log_mass_tgt, pair_blocks, pair_counts):
    sb = text_emb.shape[0] // BLK
    tb = image_emb.shape[0] // BLK
    width = text_emb.shape[1]
    cap = pair_blocks.shape[0]
    inner = 2 if n_src % 2 == 0 else 1
    n_outer = n_src // inner
    tgt_own = tb * BLK // n_src
    src_own = sb * BLK // n_tgt

    slot_ids = jnp.arange(cap, dtype=jnp.int32)
    combo = pair_blocks[:, 0] * tb + pair_blocks[:, 1]
    codes = combo + jnp.where(slot_ids < pair_counts[0], 0, sb * tb)
    combos = jnp.arange(sb * tb, dtype=jnp.int32)
    slots = jnp.min(jnp.where(codes[None, :] == combos[:, None], slot_ids[None, :], cap), axis=1)

    f32, bf16 = jnp.float32, jnp.bfloat16
    dma = pltpu.SemaphoreType.DMA
    smem = pl.BlockSpec(memory_space=pltpu.SMEM)
    vmem = pl.BlockSpec(memory_space=pltpu.VMEM)
    return pl.pallas_call(
        functools.partial(kernel, n_src, n_tgt, inner),
        out_shape=(
            jax.ShapeDtypeStruct((src_own, width), f32),
            jax.ShapeDtypeStruct((tgt_own, width), f32),
        ),
        in_specs=[smem] * 2 + [pl.BlockSpec(memory_space=pltpu.HBM)] * 4,
        out_specs=(vmem, vmem),
        scratch_shapes=[
            pltpu.VMEM((sb, BLK, width), bf16),
            pltpu.VMEM((tb, BLK, width), bf16),
            pltpu.VMEM((sb * BLK // LANES, LANES), f32),
            pltpu.VMEM((tb * BLK // LANES, LANES), f32),
            pltpu.VMEM((sb, BLK), f32),
            pltpu.VMEM((tb, BLK), f32),
            pltpu.VMEM((cap, BLK, BLK), f32),
            pltpu.VMEM((cap, BLK, BLK), f32),
            pltpu.VMEM((cap + 1, BLK, BLK), bf16),
            pltpu.VMEM((cap + 1, BLK, BLK), bf16),
            pltpu.VMEM((cap, sb, BLK), f32),
            pltpu.VMEM((cap, tb, BLK), f32),
            pltpu.VMEM((sb, BLK, LANES), f32),
            pltpu.VMEM((tb, BLK, LANES), f32),
            pltpu.VMEM((sb, 1, BLK), f32),
            pltpu.VMEM((tb, 1, BLK), f32),
            pltpu.VMEM((cap, 8, BLK), f32),
            pltpu.VMEM((cap, 8, BLK), f32),
            pltpu.VMEM((ITERS + 1, n_tgt, sb, BLK), f32),
            pltpu.VMEM((ITERS + 1, n_src, tb, BLK), f32),
            pltpu.VMEM((n_outer, tgt_own, width), f32),
            pltpu.VMEM((n_outer, tgt_own, width), f32),
            pltpu.VMEM((n_outer, tgt_own, width), f32),
            pltpu.VMEM((n_outer, tgt_own, width), f32),
            pltpu.VMEM((n_tgt, src_own, width), f32),
            pltpu.VMEM((n_tgt, src_own, width), f32),
            dma((ITERS + 1, n_tgt)),
            dma((ITERS + 1, n_tgt)),
            dma((ITERS + 1, n_src)),
            dma((ITERS + 1, n_src)),
            dma((n_outer, 2)),
            dma((n_outer, 2)),
            dma((n_outer, 2)),
            dma((n_outer, 2)),
            dma((n_tgt,)),
            dma((n_tgt,)),
            dma((4,)),
        ],
        compiler_params=pltpu.CompilerParams(
            collective_id=0, has_side_effects=True, vmem_limit_bytes=53 * 1024 * 1024
        ),
    )(
        codes,
        slots,
        text_emb.reshape(sb, BLK, width),
        image_emb.reshape(tb, BLK, width),
        log_mass_src.reshape(-1, LANES),
        log_mass_tgt.reshape(-1, LANES),
    )


def solution(mesh):
    n_src, n_tgt = mesh.shape["src"], mesh.shape["tgt"]
    return jax.shard_map(
        functools.partial(local, n_src, n_tgt),
        mesh=mesh,
        in_specs=(
            P("src", None),
            P("tgt", None),
            P("src"),
            P("tgt"),
            P(("src", "tgt"), None),
            P(("src", "tgt")),
        ),
        out_specs=(P(("src", "tgt"), None), P(("tgt", "src"), None)),
        check_vma=False,
    )
```
